768 devices in a mesh: row: 48 (over z, x_lo, core), col: 16 (over x_hi, y).
Axes of the slice: x: 4 (x_hi: 2, x_lo: 2; x = x_hi * 2 + x_lo), y: 8, z: 12, core: 2. Of those that a mesh axis runs over, the one named last changes fastest.
Arguments:
- master_weight: float32 [12288, 12288], P('col', 'row'), may hold values from -3 to 3
- gradient: bfloat16 [12288, 12288], P('col', 'row'), may hold values from -6 to 6
- first_moment: float32 [768, 12288], P('row', 'col'), may hold values from -4 to 4
- second_moment: float32 [768, 12288], P('row', 'col'), may hold values from 0.05 to 2
- left_basis: float32 [12288, 768], P('col'), may hold values from -0.0546875 to 0.0546875
- right_basis: float32 [12288, 12288], P('row', 'col'), may hold values from -0.0546875 to 0.0546875
Outputs:
- new_weight: bfloat16 [12288, 12288], P('col', 'row')
- direction: float32 [12288, 12288], P('col', 'row')
- new_first: float32 [768, 12288], P('row', 'col')
- new_second: float32 [768, 12288], P('row', 'col')
The draws below stay inside these ranges and needn't reach their ends.
All inputs are finite; a program needn't handle non-finite values.
Results may differ from the reference program's by a relative error of at most 0.001.
Values sent between devices are 32-bit elements; how exact they have to be, the bound alone decides.
No kernel may reach another device: no remote copies, remote signals or barrier semaphores. Data moves between devices by JAX's collectives and lax.ppermute only.
A program may use at most 32 MiB of HBM per device.

```python
import math
import jax
import jax.numpy as jnp
from jax import lax

ROWS = 12288
COLS = 12288
STEP = 10
WINDOW = 768


def block_levels(own_key, dims, split, least, largest):
    def one(axis_at, shards_of):
        steps = jax.random.uniform(jax.random.fold_in(jax.random.fold_in(own_key, 6), axis_at), (shards_of,), jnp.float32, least / len(split), largest / len(split))
        return jnp.repeat(jnp.exp(steps), dims[axis_at] // shards_of).reshape((-1,) + (1,) * (len(dims) - axis_at - 1))

    level = one(*split[0])
    for cut in split[1:]:
        level = level * one(*cut)
    return level


def gaussian(key, dims, scale, reach, pieces=(), kind=jnp.bfloat16):
    array = scale * jax.random.normal(key, dims, jnp.float32)
    if pieces:
        array = array * block_levels(key, dims, pieces, -0.22, 0.18)
    return jnp.clip(array, -reach, reach).astype(kind)


def setup_inputs(seed: int = 0) -> dict:
    arg_keys = jax.random.split(jax.random.key(seed), 7)
    master_weight = gaussian(arg_keys[0], (ROWS, COLS), 0.5, 3.0, ((0, 16), (1, 48)), jnp.float32)
    gradient = gaussian(arg_keys[1], (ROWS, COLS), 1.0, 6.0, ((0, 16), (1, 48)))
    first_moment = gaussian(arg_keys[2], (WINDOW, COLS), 0.5, 4.0, ((0, 48), (1, 16)), jnp.float32)
    second_moment = jnp.clip(jnp.exp(math.log(2.0) - 3.6888794 * jax.random.uniform(arg_keys[3], (WINDOW, COLS), jnp.float32) ** block_levels(arg_keys[3], (WINDOW, COLS), ((0, 48), (1, 16)), -0.2, 0.2)), 0.05, 2.0)
    left_basis = gaussian(arg_keys[4], (ROWS, WINDOW), ROWS ** -0.5, 0.0546875, ((0, 16),), jnp.float32)
    right_basis = gaussian(arg_keys[5], (COLS, COLS), COLS ** -0.5, 0.0546875, ((0, 48), (1, 16)), jnp.float32)
    return dict(master_weight=master_weight, gradient=gradient, first_moment=first_moment, second_moment=second_moment, left_basis=left_basis, right_basis=right_basis)


def reference(master_weight, gradient, first_moment, second_moment, left_basis, right_basis):
    highest = lax.Precision.HIGHEST
    grad_full = gradient.astype(jnp.float32)
    left_rotated = jnp.dot(left_basis.T, grad_full, precision=highest)
    rotated = jnp.dot(left_rotated, right_basis, precision=highest)
    new_first = 0.95 * first_moment + 0.05 * rotated
    new_second = 0.95 * second_moment + 0.05 * rotated * rotated
    correction = 1.0 - 0.95 ** STEP
    normed = new_first / correction / (jnp.sqrt(new_second / correction) + 1e-08)
    back = jnp.dot(normed, right_basis.T, precision=highest)
    direction = jnp.dot(left_basis, back, precision=highest)
    new_weight = (master_weight - 0.003 * (direction + 0.1 * master_weight)).astype(jnp.bfloat16)
    return (new_weight, direction, new_first, new_second)
```

```python
import jax
import jax.numpy as jnp
from jax import lax
from jax.sharding import Mesh, PartitionSpec as P

STEP = 10
ROW = ("z", "xl", "core")
COL = ("xh", "y")
HIGH = lax.Precision.HIGH


def swap(x, axis):
    return lax.ppermute(x, axis, [(0, 1), (1, 0)])


def sum_over_col(part):
    count = lax.axis_size("y")
    pieces = part.reshape(count, part.shape[0] // count, part.shape[1])
    mine = jnp.sum(lax.all_to_all(pieces, "y", 0, 0, tiled=True), axis=0)
    mine = mine + swap(mine, "xh")
    return lax.all_gather(mine, "y", axis=0, tiled=True)


def shards(master_weight, gradient, first_moment, second_moment, left_basis, right_basis):
    own, cols = first_moment.shape
    depth = lax.axis_size("z")
    keys = gradient.shape[1]
    core = lax.axis_index("core")
    correction = 1.0 - 0.95**STEP

    partial_left = lax.dot_general(
        left_basis, gradient.astype(jnp.float32), (((0,), (0,)), ((), ())), precision=HIGH
    )
    left_rotated = sum_over_col(partial_left)

    grouped = left_rotated.reshape(depth, 2, 2, own, keys)

    def half(which):
        picked = lax.dynamic_index_in_dim(grouped, which, 2, keepdims=False)
        picked = jnp.transpose(picked, (1, 0, 2, 3)).reshape(2 * depth * own, keys)
        return jnp.dot(picked, right_basis, precision=HIGH)

    theirs = swap(half(1 - core), "core")
    summed = half(core) + theirs
    pair = lax.all_to_all(summed.reshape(2, depth * own, cols), "xl", 0, 0, tiled=True)
    summed = (pair[0] + pair[1]).reshape(depth, own, cols)
    rotated = jnp.sum(lax.all_to_all(summed, "z", 0, 0, tiled=True), axis=0)

    new_first = 0.95 * first_moment + 0.05 * rotated
    new_second = 0.95 * second_moment + 0.05 * rotated * rotated
    normed = new_first / correction / (jnp.sqrt(new_second / correction) + 1e-08)

    column = lax.all_gather(normed, "z", axis=0, tiled=True)
    both = lax.all_to_all(jnp.stack([column, column]), "xl", 0, 0, tiled=True)
    mine = both.reshape(2 * depth * own, cols)
    other = swap(mine, "core")
    contract = (((1,), (1,)), ((), ()))
    back_part = jnp.concatenate(
        [
            lax.dot_general(mine, right_basis, contract, precision=HIGH),
            lax.dot_general(other, right_basis, contract, precision=HIGH),
        ]
    )
    back = sum_over_col(back_part).reshape(2, 2, depth, own, keys)
    back = jnp.where(core == 0, back, back[::-1])
    back = jnp.transpose(back, (2, 1, 0, 3, 4)).reshape(back_part.shape)
    direction = jnp.dot(left_basis, back, precision=HIGH)
    new_weight = (master_weight - 0.003 * (direction + 0.1 * master_weight)).astype(jnp.bfloat16)
    return (new_weight, direction, new_first, new_second)


def solution(mesh):
    fine = Mesh(mesh.devices.reshape(12, 2, 2, 2, 8), ROW + COL)
    in_specs = (P(COL, ROW), P(COL, ROW), P(ROW, COL), P(ROW, COL), P(COL, None), P(ROW, COL))
    out_specs = (P(COL, ROW), P(COL, ROW), P(ROW, COL), P(ROW, COL))
    return jax.shard_map(shards, mesh=fine, in_specs=in_specs, out_specs=out_specs, check_vma=False)
```

```python
import jax
import jax.numpy as jnp
from jax import lax
from jax.sharding import Mesh, PartitionSpec as P

STEP = 10
ROW = ("z", "xl", "core")
COL = ("xh", "y")
HIGH = lax.Precision.HIGH


def swap(x, axis):
    return lax.ppermute(x, axis, [(0, 1), (1, 0)])


def scatter_sum(x, axes):
    return jnp.sum(lax.all_to_all(x, axes, 0, 0, tiled=True), axis=0)


def gather(x, axes):
    copies = jnp.broadcast_to(x[None], (lax.axis_size(axes),) + x.shape)
    return lax.all_to_all(copies, axes, 0, 0, tiled=True)


def shards(master_weight, gradient, first_moment, second_moment, left_basis, right_basis):
    own, cols = first_moment.shape
    window = left_basis.shape[1]
    depth = lax.axis_size("z")
    peers = lax.axis_size(COL)
    piece = window // 2 // peers
    keys = gradient.shape[1]
    core = lax.axis_index("core")
    xl = lax.axis_index("xl")
    correction = 1.0 - 0.95**STEP

    basis = jnp.concatenate([right_basis, swap(right_basis, "xl")], axis=0)

    partial_left = lax.dot_general(
        left_basis, gradient.astype(jnp.float32), (((0,), (0,)), ((), ())), precision=HIGH
    )
    parts = partial_left.reshape(depth, 2, 2 * own, keys).transpose(1, 0, 2, 3)
    parts = parts.reshape(2, peers, piece, keys).transpose(1, 0, 2, 3)
    mine, basis = lax.optimization_barrier((scatter_sum(parts, COL), basis))
    keep = lax.dynamic_index_in_dim(mine, xl, 0, keepdims=False)
    got = swap(lax.dynamic_index_in_dim(mine, 1 - xl, 0, keepdims=False), "xl")
    left_rotated = gather(jnp.concatenate([keep, got], axis=1), COL)
    grouped = left_rotated.reshape(depth, 2, own, 2 * keys)

    def half(which):
        picked = lax.dynamic_index_in_dim(grouped, which, 1, keepdims=False)
        return jnp.dot(picked.reshape(depth * own, 2 * keys), basis, precision=HIGH)

    theirs = swap(half(1 - core), "core")
    summed = half(core) + theirs
    rotated = scatter_sum(summed.reshape(depth, own, cols), "z")

    new_first = 0.95 * first_moment + 0.05 * rotated
    new_second = 0.95 * second_moment + 0.05 * rotated * rotated
    normed = new_first / correction / (jnp.sqrt(new_second / correction) + 1e-08)

    column = lax.all_gather(normed, "z", axis=0, tiled=True)
    other = swap(column, "core")
    contract = (((1,), (1,)), ((), ()))
    back_part = jnp.concatenate(
        [
            lax.dot_general(column, basis, contract, precision=HIGH),
            lax.dot_general(other, basis, contract, precision=HIGH),
        ]
    )
    mine = scatter_sum(back_part.reshape(peers, piece, 2 * keys), COL)
    keep, got = mine[:, :keys], swap(mine[:, keys:], "xl")
    pair = jnp.where(xl == 0, jnp.stack([keep, got]), jnp.stack([got, keep]))
    back = gather(pair, COL).transpose(1, 0, 2, 3).reshape(2, 2, depth, own, keys)
    back = jnp.where(core == 0, back, back[:, ::-1])
    back = back.transpose(2, 0, 1, 3, 4).reshape(window, keys)
    direction = jnp.dot(left_basis, back, precision=HIGH)
    new_weight = (master_weight - 0.003 * (direction + 0.1 * master_weight)).astype(jnp.bfloat16)
    return (new_weight, direction, new_first, new_second)


def solution(mesh):
    fine = Mesh(mesh.devices.reshape(12, 2, 2, 2, 8), ROW + COL)
    in_specs = (P(COL, ROW), P(COL, ROW), P(ROW, COL), P(ROW, COL), P(COL, None), P(ROW, COL))
    out_specs = (P(COL, ROW), P(COL, ROW), P(ROW, COL), P(ROW, COL))
    return jax.shard_map(shards, mesh=fine, in_specs=in_specs, out_specs=out_specs, check_vma=False)
```

```python
import jax
import jax.numpy as jnp
from jax import lax
from jax.sharding import Mesh, PartitionSpec as P

STEP = 10
ROW = ("z", "xl", "core")
COL = ("xh", "y")
HIGH = lax.Precision.HIGH


def swap(x, axis):
    return lax.ppermute(x, axis, [(0, 1), (1, 0)])


def cross(x):
    return lax.ppermute(x, ("xl", "xh"), [(0, 3), (3, 0), (1, 2), (2, 1)])


def exchange(x, axes):
    return lax.all_to_all(x, axes, 0, 0, tiled=True)


def mine_first(x, index):
    return jnp.where(index == 0, x, x[::-1])


def shards(master_weight, gradient, first_moment, second_moment, left_basis, right_basis):
    own, cols = first_moment.shape
    window = left_basis.shape[1]
    depth = lax.axis_size("z")
    peers = lax.axis_size("y")
    few = own // 2
    piece = window // 4 // peers
    keys = gradient.shape[1]
    core, xl, xh = lax.axis_index("core"), lax.axis_index("xl"), lax.axis_index("xh")
    correction = 1.0 - 0.95**STEP

    by_xl, by_both = swap(right_basis, "xl"), cross(right_basis)

    partial_left = lax.dot_general(
        left_basis, gradient.astype(jnp.float32), (((0,), (0,)), ((), ())), precision=HIGH
    )
    parts = partial_left.reshape(depth, 2, 2, 2, few, keys).transpose(1, 3, 0, 2, 4, 5)
    parts = exchange(parts.reshape(4 * peers, piece, keys), ("xl", "xh", "y"))
    parts, by_xl, by_both = lax.optimization_barrier((parts, by_xl, by_both))
    left_chunk = jnp.sum(parts.reshape(2, 2 * peers, piece, keys), axis=1)
    left_chunk = mine_first(left_chunk, xl).transpose(1, 0, 2).reshape(piece, 2 * keys)
    left_rotated = exchange(jnp.broadcast_to(left_chunk[None], (peers, piece, 2 * keys)), "y")

    middle = right_basis.shape[0] // 2
    by_xh = jnp.concatenate([swap(by_both[:middle], "xl"), cross(by_xl[middle:])])
    basis_own = jnp.concatenate([right_basis, by_xl])
    basis_other = jnp.concatenate([by_xh, by_both])

    grouped = left_rotated.reshape(depth, 2, few, 2 * keys)

    def half(which):
        picked = lax.dynamic_index_in_dim(grouped, which, 1, keepdims=False)
        picked = picked.reshape(depth * few, 2 * keys)
        return jnp.stack(
            [jnp.dot(picked, basis_own, precision=HIGH), jnp.dot(picked, basis_other, precision=HIGH)]
        )

    theirs = swap(half(1 - core), "core")
    summed = mine_first(half(core) + theirs, xh).reshape(2, depth, few, cols)
    summed = summed.transpose(1, 0, 2, 3).reshape(2 * depth, few, cols)
    rotated = jnp.sum(exchange(summed, ("z", "xh")).reshape(depth, own, cols), axis=0)

    new_first = 0.95 * first_moment + 0.05 * rotated
    new_second = 0.95 * second_moment + 0.05 * rotated * rotated
    normed = new_first / correction / (jnp.sqrt(new_second / correction) + 1e-08)

    copies = jnp.broadcast_to(normed.reshape(1, 2, few, cols), (depth, 2, few, cols))
    column = exchange(copies.reshape(2 * depth, few, cols), ("z", "xh"))
    other = swap(column, "core")
    contract = (((1,), (1,)), ((), ()))

    def rotate_back(x):
        x = x.reshape(depth, 2, few, cols).transpose(1, 0, 2, 3).reshape(2, depth * few, cols)
        x = mine_first(x, xh)
        return lax.dot_general(x[0], basis_own, contract, precision=HIGH) + lax.dot_general(
            x[1], basis_other, contract, precision=HIGH
        )

    back_part = jnp.concatenate([rotate_back(column), rotate_back(other)])
    back_part = back_part.reshape(peers, piece, 2, keys).transpose(2, 0, 1, 3)
    back_part = mine_first(back_part, xl).reshape(2 * peers, piece, keys)
    back_chunk = exchange(back_part, ("xl", "y")).reshape(2, peers, piece, keys)
    back_chunk = jnp.sum(back_chunk, axis=1)
    copies = jnp.broadcast_to(back_chunk[None], (2 * peers, 2, piece, keys))
    back = exchange(copies, COL).reshape(2, peers, 2, piece, keys).transpose(0, 2, 1, 3, 4)
    back = back.reshape(2, 2, 2, depth, few, keys)
    back = jnp.where(core == 0, back, back[:, :, ::-1])
    back = back.transpose(3, 1, 2, 0, 4, 5).reshape(window, keys)
    direction = jnp.dot(left_basis, back, precision=HIGH)
    new_weight = (master_weight - 0.003 * (direction + 0.1 * master_weight)).astype(jnp.bfloat16)
    return (new_weight, direction, new_first, new_second)


def solution(mesh):
    fine = Mesh(mesh.devices.reshape(12, 2, 2, 2, 8), ROW + COL)
    in_specs = (P(COL, ROW), P(COL, ROW), P(ROW, COL), P(ROW, COL), P(COL, None), P(ROW, COL))
    out_specs = (P(COL, ROW), P(COL, ROW), P(ROW, COL), P(ROW, COL))
    return jax.shard_map(shards, mesh=fine, in_specs=in_specs, out_specs=out_specs, check_vma=False)
```

```python
import jax
import jax.numpy as jnp
from jax import lax
from jax.sharding import Mesh, PartitionSpec as P

STEP = 10
ROW = ("z", "xl", "core")
COL = ("xh", "y")
HIGH = lax.Precision.HIGH


def swap(x, axis):
    return lax.ppermute(x, axis, [(0, 1), (1, 0)])


def exchange(x, axes):
    return lax.all_to_all(x, axes, 0, 0, tiled=True)


def shards(master_weight, gradient, first_moment, second_moment, left_basis, right_basis):
    own, cols = first_moment.shape
    window = left_basis.shape[1]
    depth = lax.axis_size("z")
    peers = lax.axis_size("y")
    few = own // 2
    piece = window // 4 // peers
    keys = gradient.shape[1]
    core = lax.axis_index("core")
    correction = 1.0 - 0.95**STEP

    basis = lax.all_gather(right_basis, ("xh", "xl"), axis=0, tiled=True)
    basis = basis.reshape(2, 2, keys, cols).swapaxes(0, 1)

    partial_left = lax.dot_general(
        left_basis, gradient.astype(jnp.float32), (((0,), (0,)), ((), ())), precision=HIGH
    )
    parts = partial_left.reshape(depth, 2, 2, 2, few, keys).transpose(1, 3, 0, 2, 4, 5)
    parts = exchange(parts.reshape(4 * peers, piece, keys), ("xl", "xh", "y"))
    left_chunk = jnp.sum(parts.reshape(2, 2 * peers, piece, keys), axis=1)
    left_chunk = left_chunk.transpose(1, 0, 2).reshape(piece, 2 * keys)
    left_rotated = exchange(jnp.broadcast_to(left_chunk[None], (peers, piece, 2 * keys)), "y")
    grouped = left_rotated.reshape(depth, 2, few, 2, keys)

    def half(which):
        picked = lax.dynamic_index_in_dim(grouped, which, 1, keepdims=False)
        picked = picked.reshape(depth * few, 2, keys)

        def block(xh):
            return jnp.dot(picked[:, 0], basis[0, xh], precision=HIGH) + jnp.dot(
                picked[:, 1], basis[1, xh], precision=HIGH
            )

        return jnp.stack([block(0), block(1)])

    theirs = swap(half(1 - core), "core")
    summed = (half(core) + theirs).reshape(2, depth, few, cols)
    summed = summed.transpose(1, 0, 2, 3).reshape(2 * depth, few, cols)
    rotated = jnp.sum(exchange(summed, ("z", "xh")).reshape(depth, own, cols), axis=0)

    new_first = 0.95 * first_moment + 0.05 * rotated
    new_second = 0.95 * second_moment + 0.05 * rotated * rotated
    normed = new_first / correction / (jnp.sqrt(new_second / correction) + 1e-08)

    copies = jnp.broadcast_to(normed.reshape(1, 2, few, cols), (depth, 2, few, cols))
    column = exchange(copies.reshape(2 * depth, few, cols), ("z", "xh"))
    other = swap(column, "core")
    contract = (((1,), (1,)), ((), ()))

    def rotate_back(x):
        x = x.reshape(depth, 2, few, cols).transpose(1, 0, 2, 3).reshape(2, depth * few, cols)

        def block(xl):
            return lax.dot_general(x[0], basis[xl, 0], contract, precision=HIGH) + lax.dot_general(
                x[1], basis[xl, 1], contract, precision=HIGH
            )

        return jnp.stack([block(0), block(1)])

    back_part = jnp.concatenate([rotate_back(column), rotate_back(other)], axis=1)
    back_part = back_part.reshape(2 * peers, piece, keys)
    back_chunk = exchange(back_part, ("xl", "y")).reshape(2, peers, piece, keys)
    back_chunk = jnp.sum(back_chunk, axis=1)
    copies = jnp.broadcast_to(back_chunk[None], (2 * peers, 2, piece, keys))
    back = exchange(copies, COL).reshape(2, peers, 2, piece, keys).transpose(0, 2, 1, 3, 4)
    back = back.reshape(2, 2, 2, depth, few, keys)
    back = jnp.where(core == 0, back, back[:, :, ::-1])
    back = back.transpose(3, 1, 2, 0, 4, 5).reshape(window, keys)
    direction = jnp.dot(left_basis, back, precision=HIGH)
    new_weight = (master_weight - 0.003 * (direction + 0.1 * master_weight)).astype(jnp.bfloat16)
    return (new_weight, direction, new_first, new_second)


def solution(mesh):
    fine = Mesh(mesh.devices.reshape(12, 2, 2, 2, 8), ROW + COL)
    in_specs = (P(COL, ROW), P(COL, ROW), P(ROW, COL), P(ROW, COL), P(COL, None), P(ROW, COL))
    out_specs = (P(COL, ROW), P(COL, ROW), P(ROW, COL), P(ROW, COL))
    return jax.shard_map(shards, mesh=fine, in_specs=in_specs, out_specs=out_specs, check_vma=False)
```

```python
import jax
import jax.numpy as jnp
from jax import lax
from jax.experimental import pallas as pl
from jax.experimental.pallas import tpu as pltpu
from jax.sharding import Mesh, PartitionSpec as P

STEP = 10
LANES = 128
ROW = ("z", "xl", "core")
COL = ("xh", "y")


def exchange(x, axes):
    return lax.all_to_all(x, axes, 0, 0, tiled=True)


def copies_to(x, axes):
    return exchange(jnp.broadcast_to(x[None], (lax.axis_size(axes),) + x.shape), axes)


def split(x):
    high = x.astype(jnp.bfloat16)
    return high, (x - high.astype(jnp.float32)).astype(jnp.bfloat16)


def three_passes(a, b, contract):
    a_high, a_low = a
    b_high, b_low = b

    def one(x, y):
        return lax.dot_general(x, y, (contract, ((), ())), preferred_element_type=jnp.float32)

    return one(a_high, b_high) + (one(a_high, b_low) + one(a_low, b_high))


def start_kernel(left_ref, gradient_ref, out_ref, total, rows):
    step = pl.program_id(0)
    high, low = split(left_ref[...])

    def one(x):
        return lax.dot_general(
            x, gradient_ref[...], (((0,), (0,)), ((), ())), preferred_element_type=jnp.float32
        )

    part = one(high) + one(low)

    @pl.when(step == 0)
    def _():
        total[...] = part

    @pl.when(step > 0)
    def _():
        total[...] += part

    @pl.when(step == pl.num_programs(0) - 1)
    def _():
        peers, piece, few = out_ref.shape[2], out_ref.shape[3] // 2, 8
        for ring in range(4):
            for xh in range(2):
                for z in range(total.shape[0] // 64):
                    at = 64 * z + 16 * ring + few * xh
                    rows[few * z : few * (z + 1), :] = total[at : at + few, :]
                for y in range(peers):
                    for part_of in range(2):
                        out_ref[ring, xh, y, piece * part_of : piece * (part_of + 1), :] = rows[
                            piece * y : piece * (y + 1), LANES * part_of : LANES * (part_of + 1)
                        ]


def start(left_basis, gradient, peers):
    height, window = left_basis.shape
    keys = gradient.shape[1]
    block = height // 3
    shape = (4, 2, peers, window // 8 // peers * (keys // LANES), LANES)
    return pl.pallas_call(
        start_kernel,
        grid=(3,),
        in_specs=[
            pl.BlockSpec((block, window), lambda i: (i, 0)),
            pl.BlockSpec((block, keys), lambda i: (i, 0)),
        ],
        out_specs=pl.BlockSpec(shape, lambda i: (0,) * 5),
        out_shape=jax.ShapeDtypeStruct(shape, jnp.float32),
        scratch_shapes=[
            pltpu.VMEM((window, keys), jnp.float32),
            pltpu.VMEM((window // 8, keys), jnp.float32),
        ],
        compiler_params=pltpu.CompilerParams(vmem_limit_bytes=60 * 2**20),
        cost_estimate=pl.CostEstimate(
            flops=4 * height * window * keys, bytes_accessed=4_000_000, transcendentals=0
        ),
    )(left_basis, gradient)


def forth_kernel(left_ref, basis_ref, out_ref, rows, high, low):
    @pl.when((pl.program_id(0) == 0) & (pl.program_id(1) == 0))
    def _():
        peers, tiles = left_ref.shape[0], rows.shape[1] // LANES
        piece = left_ref.shape[1] // tiles
        for y in range(peers):
            for tile in range(tiles):
                rows[piece * y : piece * (y + 1), LANES * tile : LANES * (tile + 1)] = left_ref[
                    y, piece * tile : piece * (tile + 1), :
                ]
        high[...], low[...] = split(rows[...])

    out_ref[...] = three_passes((high[...], low[...]), split(basis_ref[0]), ((1,), (0,)))


def forth(left, basis):
    halves, keys, cols = basis.shape
    count = left.shape[0] * left.shape[1] * LANES // keys
    block = cols // 3
    return pl.pallas_call(
        forth_kernel,
        grid=(halves, 3),
        in_specs=[
            pl.BlockSpec(left.shape, lambda i, j: (0, 0, 0)),
            pl.BlockSpec((1, keys, block), lambda i, j: (i, 0, j)),
        ],
        out_specs=pl.BlockSpec((count, block), lambda i, j: (0, 3 * i + j)),
        out_shape=jax.ShapeDtypeStruct((count, halves * cols), jnp.float32),
        scratch_shapes=[
            pltpu.VMEM((count, keys), jnp.float32),
            pltpu.VMEM((count, keys), jnp.bfloat16),
            pltpu.VMEM((count, keys), jnp.bfloat16),
        ],
        compiler_params=pltpu.CompilerParams(vmem_limit_bytes=57 * 2**20),
        cost_estimate=pl.CostEstimate(
            flops=6 * count * keys * halves * cols, bytes_accessed=8_000_000, transcendentals=0
        ),
    )(left, basis)


def back_kernel(column_ref, basis_ref, out_ref, rows, high, low):
    @pl.when(pl.program_id(0) == 0)
    def _():
        high[...], low[...] = split(column_ref[...])

    cols = basis_ref.shape[2]
    contract = ((1,), (1,))
    first, second = (
        three_passes(
            (high[:, cols * i : cols * (i + 1)], low[:, cols * i : cols * (i + 1)]),
            split(basis_ref[i]),
            contract,
        )
        for i in range(2)
    )
    rows[...] = first + second
    peers, piece = out_ref.shape[1], out_ref.shape[2] // 2
    for y in range(peers):
        for part in range(2):
            out_ref[0, y, piece * part : piece * (part + 1), :] = rows[
                piece * y : piece * (y + 1), LANES * part : LANES * (part + 1)
            ]


def rotate_back(column, basis, peers):
    halves, keys, cols = basis.shape
    count = column.shape[0]
    block = keys // 4
    shape = (4, peers, count // peers * (block // LANES), LANES)
    return pl.pallas_call(
        back_kernel,
        grid=(4,),
        in_specs=[
            pl.BlockSpec(column.shape, lambda i: (0, 0)),
            pl.BlockSpec((halves, block, cols), lambda i: (0, i, 0)),
        ],
        out_specs=pl.BlockSpec((1,) + shape[1:], lambda i: (i, 0, 0, 0)),
        out_shape=jax.ShapeDtypeStruct(shape, jnp.float32),
        scratch_shapes=[
            pltpu.VMEM((count, block), jnp.float32),
            pltpu.VMEM(column.shape, jnp.bfloat16),
            pltpu.VMEM(column.shape, jnp.bfloat16),
        ],
        compiler_params=pltpu.CompilerParams(vmem_limit_bytes=57 * 2**20),
        cost_estimate=pl.CostEstimate(
            flops=6 * count * keys * halves * cols, bytes_accessed=8_000_000, transcendentals=0
        ),
    )(column, basis)


def finish_kernel(got_ref, left_ref, master_ref, weight_ref, direction_ref, rows, back, high, low):
    peers, few = got_ref.shape[1], 8
    piece = got_ref.shape[3] // 2
    depth = back.shape[0] // 64

    @pl.when(pl.program_id(0) == 0)
    def _():
        for xh in range(2):
            for ring in range(4):
                for y in range(peers):
                    for part in range(2):
                        rows[piece * y : piece * (y + 1), LANES * part : LANES * (part + 1)] = got_ref[
                            xh, y, ring, piece * part : piece * (part + 1), :
                        ]
                for z in range(depth):
                    at = 64 * z + 16 * ring + few * xh
                    back[at : at + few, :] = rows[few * z : few * (z + 1), :]
        high[...], low[...] = split(back[...])

    step = three_passes(split(left_ref[...]), (high[...], low[...]), ((1,), (0,)))
    master = master_ref[...]
    direction_ref[...] = step
    weight_ref[...] = (master - 0.003 * (step + 0.1 * master)).astype(jnp.bfloat16)


def finish(got, left_basis, master_weight):
    height, keys = master_weight.shape
    window = left_basis.shape[1]
    block = height // 4
    by_rows = pl.BlockSpec((block, keys), lambda i: (i, 0))
    return pl.pallas_call(
        finish_kernel,
        grid=(4,),
        in_specs=[
            pl.BlockSpec(got.shape, lambda i: (0,) * got.ndim),
            pl.BlockSpec((block, window), lambda i: (i, 0)),
            by_rows,
        ],
        out_specs=[by_rows, by_rows],
        out_shape=[
            jax.ShapeDtypeStruct((height, keys), jnp.bfloat16),
            jax.ShapeDtypeStruct((height, keys), jnp.float32),
        ],
        scratch_shapes=[
            pltpu.VMEM((window // 8, keys), jnp.float32),
            pltpu.VMEM((window, keys), jnp.float32),
            pltpu.VMEM((window, keys), jnp.bfloat16),
            pltpu.VMEM((window, keys), jnp.bfloat16),
        ],
        compiler_params=pltpu.CompilerParams(vmem_limit_bytes=24 * 2**20),
        cost_estimate=pl.CostEstimate(
            flops=6 * height * window * keys, bytes_accessed=6_000_000, transcendentals=0
        ),
    )(got, left_basis, master_weight)


def shards(master_weight, gradient, first_moment, second_moment, left_basis, right_basis):
    own, cols = first_moment.shape
    depth = lax.axis_size("z")
    peers = lax.axis_size("y")
    few = own // 2
    keys = gradient.shape[1]
    xh = lax.axis_index("xh")
    correction = 1.0 - 0.95**STEP

    def in_order(mine, other, axis):
        pair = jnp.stack([mine, other], axis=axis)
        return jnp.where(xh == 0, pair, jnp.stack([other, mine], axis=axis))

    def trade(x, axis):
        mine = lax.dynamic_index_in_dim(x, xh, axis, keepdims=False)
        other = lax.dynamic_index_in_dim(x, 1 - xh, axis, keepdims=False)
        return mine, lax.ppermute(other, "xh", [(0, 1), (1, 0)])

    basis = lax.all_gather(right_basis, ("xh", "xl", "core"), axis=0, tiled=True)
    basis = basis.reshape(2, 4 * keys, cols)
    moments = jnp.stack([first_moment, second_moment]).reshape(2, 2, few, cols)
    moments = in_order(*trade(moments, 1), axis=2).reshape(2, few, 2 * cols)

    parts = start(left_basis, gradient, peers)
    parts = exchange(parts.reshape((-1,) + parts.shape[3:]), ("xl", "core", "xh", "y"))
    left_chunk = jnp.sum(parts.reshape(4, 2 * peers, -1, LANES), axis=1).reshape(-1, LANES)
    left_rotated = copies_to(left_chunk, "y")

    summed = forth(left_rotated, basis).reshape(depth, few, 2 * cols)
    rotated = jnp.sum(exchange(summed, "z"), axis=0)

    new_first = 0.95 * moments[0] + 0.05 * rotated
    new_second = 0.95 * moments[1] + 0.05 * rotated * rotated
    normed = new_first / correction / (jnp.sqrt(new_second / correction) + 1e-08)

    column = copies_to(normed, "z").reshape(depth * few, 2 * cols)
    moments = jnp.stack([new_first, new_second]).reshape(2, few, 2, cols)
    moments = in_order(*trade(moments, 2), axis=1).reshape(2, own, cols)

    back_part = rotate_back(column, basis, peers)
    back_part = exchange(back_part.reshape((-1,) + back_part.shape[2:]), ("xl", "core", "y"))
    back_chunk = jnp.sum(back_part.reshape((4, peers) + back_part.shape[1:]), axis=1)
    got = copies_to(back_chunk, COL).reshape((2, peers) + back_chunk.shape)
    new_weight, direction = finish(got, left_basis, master_weight)
    return (new_weight, direction, moments[0], moments[1])


def solution(mesh):
    fine = Mesh(mesh.devices.reshape(12, 2, 2, 2, 8), ROW + COL)
    in_specs = (P(COL, ROW), P(COL, ROW), P(ROW, COL), P(ROW, COL), P(COL, None), P(ROW, COL))
    out_specs = (P(COL, ROW), P(COL, ROW), P(ROW, COL), P(ROW, COL))
    return jax.shard_map(shards, mesh=fine, in_specs=in_specs, out_specs=out_specs, check_vma=False)
```

```python
import jax
import jax.numpy as jnp
from jax import lax
from jax.experimental import pallas as pl
from jax.experimental.pallas import tpu as pltpu
from jax.sharding import Mesh, PartitionSpec as P

STEP = 10
LANES = 128
ROW = ("z", "xl", "core")
COL = ("xh", "y")


def swap(x, axis):
    return lax.ppermute(x, axis, [(0, 1), (1, 0)])


def cross(x):
    return lax.ppermute(x, ("xl", "xh"), [(0, 3), (3, 0), (1, 2), (2, 1)])


def relay(x):
    flip = (4, 7)
    pairs = [(i, i ^ flip[(i >> 1) & 1] ^ (2 * ((i >> 1) & 1))) for i in range(8)]
    return lax.ppermute(x, ("xl", "core", "xh"), pairs)


def exchange(x, axes):
    return lax.all_to_all(x, axes, 0, 0, tiled=True)


def copies_to(x, axes):
    return exchange(jnp.broadcast_to(x[None], (lax.axis_size(axes),) + x.shape), axes)


def split(x):
    high = x.astype(jnp.bfloat16)
    return high, (x - high.astype(jnp.float32)).astype(jnp.bfloat16)


def three_passes(a, b, contract):
    a_high, a_low = a
    b_high, b_low = b

    def one(x, y):
        return lax.dot_general(x, y, (contract, ((), ())), preferred_element_type=jnp.float32)

    return one(a_high, b_high) + (one(a_high, b_low) + one(a_low, b_high))


def start_kernel(left_ref, gradient_ref, out_ref, total, rows):
    step = pl.program_id(0)
    high, low = split(left_ref[...])
    turned = gradient_ref[...].astype(jnp.float32).T.astype(jnp.bfloat16)

    def one(x):
        return jnp.dot(turned, x, preferred_element_type=jnp.float32)

    part = one(high) + one(low)

    @pl.when(step == 0)
    def _():
        total[...] = part

    @pl.when(step > 0)
    def _():
        total[...] += part

    @pl.when(step == pl.num_programs(0) - 1)
    def _():
        whole = total[...].T
        peers, piece, few = out_ref.shape[2], out_ref.shape[3] // 2, 8
        for ring in range(4):
            for xh in range(2):
                for z in range(total.shape[1] // 64):
                    at = 64 * z + 16 * ring + few * xh
                    rows[few * z : few * (z + 1), :] = whole[at : at + few, :]
                for y in range(peers):
                    for part_of in range(2):
                        out_ref[ring, xh, y, piece * part_of : piece * (part_of + 1), :] = rows[
                            piece * y : piece * (y + 1), LANES * part_of : LANES * (part_of + 1)
                        ]


def start(left_basis, gradient, peers):
    height, window = left_basis.shape
    keys = gradient.shape[1]
    block = height // 3
    shape = (4, 2, peers, window // 8 // peers * (keys // LANES), LANES)
    return pl.pallas_call(
        start_kernel,
        grid=(3,),
        in_specs=[
            pl.BlockSpec((block, window), lambda i: (i, 0)),
            pl.BlockSpec((block, keys), lambda i: (i, 0)),
        ],
        out_specs=pl.BlockSpec(shape, lambda i: (0,) * 5),
        out_shape=jax.ShapeDtypeStruct(shape, jnp.float32),
        scratch_shapes=[
            pltpu.VMEM((keys, window), jnp.float32),
            pltpu.VMEM((window // 8, keys), jnp.float32),
        ],
        compiler_params=pltpu.CompilerParams(vmem_limit_bytes=24 * 2**20),
        cost_estimate=pl.CostEstimate(
            flops=4 * height * window * keys, bytes_accessed=4_000_000, transcendentals=0
        ),
    )(left_basis, gradient)


def forth_kernel(left_ref, *refs):
    basis, (out_ref, rows, high, low) = refs[:8], refs[8:]
    keys = basis[0].shape[0]

    @pl.when(pl.program_id(0) == 0)
    def _():
        peers, tiles = left_ref.shape[0], rows.shape[1] // LANES
        piece = left_ref.shape[1] // tiles
        for y in range(peers):
            for tile in range(tiles):
                rows[piece * y : piece * (y + 1), LANES * tile : LANES * (tile + 1)] = left_ref[
                    y, piece * tile : piece * (tile + 1), :
                ]
        high[...], low[...] = split(rows[...])

    few = out_ref.shape[1] // 2
    for half in range(2):
        total = None
        for i in range(4):
            at = slice(keys * i, keys * (i + 1))
            term = three_passes(
                (high[:, at], low[:, at]), split(basis[4 * half + i][...]), ((1,), (0,))
            )
            total = term if total is None else total + term
        out_ref[:, few * half : few * (half + 1), :] = total.reshape(-1, few, total.shape[1])


def forth(left, basis, few):
    keys, cols = basis[0].shape
    count = left.shape[0] * left.shape[1] * LANES // (4 * keys)
    block = cols // 3
    depth = count // few
    return pl.pallas_call(
        forth_kernel,
        grid=(3,),
        in_specs=[pl.BlockSpec(left.shape, lambda j: (0, 0, 0))]
        + [pl.BlockSpec((keys, block), lambda j: (0, j))] * 8,
        out_specs=pl.BlockSpec((depth, 2 * few, block), lambda j: (0, 0, j)),
        out_shape=jax.ShapeDtypeStruct((depth, 2 * few, cols), jnp.float32),
        scratch_shapes=[
            pltpu.VMEM((count, 4 * keys), jnp.float32),
            pltpu.VMEM((count, 4 * keys), jnp.bfloat16),
            pltpu.VMEM((count, 4 * keys), jnp.bfloat16),
        ],
        compiler_params=pltpu.CompilerParams(vmem_limit_bytes=24 * 2**20),
        cost_estimate=pl.CostEstimate(
            flops=48 * count * keys * cols, bytes_accessed=8_000_000, transcendentals=0
        ),
    )(left, *basis)


def back_kernel(me_ref, column_ref, *refs):
    basis, (out_ref, rows, whole, high, low) = refs[:8], refs[8:]
    few = column_ref.shape[1] // 2
    step = pl.program_id(0)

    @pl.when(step == 0)
    def _():
        for half in range(2):
            for z in range(column_ref.shape[0]):
                whole[half, few * z : few * (z + 1), :] = column_ref[
                    z, few * half : few * (half + 1), :
                ]
        high[...], low[...] = split(whole[...])

    peers, piece = out_ref.shape[1], out_ref.shape[2] // 2
    for i in range(4):
        first, second = (
            three_passes((high[half], low[half]), split(basis[4 * half + i][...]), ((1,), (1,)))
            for half in range(2)
        )
        rows[i] = first + second
    for part in range(2):

        @pl.when(step == part)
        def _():
            for i in range(4):
                ring = jnp.bitwise_xor(me_ref[0], i)
                for y in range(peers):
                    out_ref[ring, y, piece * part : piece * (part + 1), :] = rows[
                        i, piece * y : piece * (y + 1), :
                    ]


def rotate_back(me, column, basis, peers):
    keys, cols = basis[0].shape
    depth, both, _ = column.shape
    count = depth * both // 2
    shape = (4, peers, 2 * count // peers, LANES)
    return pl.pallas_call(
        back_kernel,
        grid=(2,),
        in_specs=[
            pl.BlockSpec(memory_space=pltpu.SMEM),
            pl.BlockSpec(column.shape, lambda i: (0, 0, 0)),
        ]
        + [pl.BlockSpec((LANES, cols), lambda i: (i, 0))] * 8,
        out_specs=pl.BlockSpec(shape, lambda i: (0, 0, 0, 0)),
        out_shape=jax.ShapeDtypeStruct(shape, jnp.float32),
        scratch_shapes=[
            pltpu.VMEM((4, count, LANES), jnp.float32),
            pltpu.VMEM((2, count, cols), jnp.float32),
            pltpu.VMEM((2, count, cols), jnp.bfloat16),
            pltpu.VMEM((2, count, cols), jnp.bfloat16),
        ],
        compiler_params=pltpu.CompilerParams(vmem_limit_bytes=24 * 2**20),
        cost_estimate=pl.CostEstimate(
            flops=48 * count * keys * cols, bytes_accessed=8_000_000, transcendentals=0
        ),
    )(me, column, *basis)


def finish_kernel(got_ref, left_ref, master_ref, weight_ref, direction_ref, rows, back, high, low):
    peers, few = got_ref.shape[1], 8
    piece = got_ref.shape[3] // 2
    depth = back.shape[0] // 64

    @pl.when(pl.program_id(0) == 0)
    def _():
        for xh in range(2):
            for ring in range(4):
                for y in range(peers):
                    for part in range(2):
                        rows[piece * y : piece * (y + 1), LANES * part : LANES * (part + 1)] = got_ref[
                            xh, y, ring, piece * part : piece * (part + 1), :
                        ]
                for z in range(depth):
                    at = 64 * z + 16 * ring + few * xh
                    back[at : at + few, :] = rows[few * z : few * (z + 1), :]
        high[...], low[...] = split(back[...])

    step = three_passes(split(left_ref[...]), (high[...], low[...]), ((1,), (0,)))
    master = master_ref[...]
    direction_ref[...] = step
    weight_ref[...] = (master - 0.003 * (step + 0.1 * master)).astype(jnp.bfloat16)


def finish(got, left_basis, master_weight):
    height, keys = master_weight.shape
    window = left_basis.shape[1]
    block = height // 4
    by_rows = pl.BlockSpec((block, keys), lambda i: (i, 0))
    return pl.pallas_call(
        finish_kernel,
        grid=(4,),
        in_specs=[
            pl.BlockSpec(got.shape, lambda i: (0,) * got.ndim),
            pl.BlockSpec((block, window), lambda i: (i, 0)),
            by_rows,
        ],
        out_specs=[by_rows, by_rows],
        out_shape=[
            jax.ShapeDtypeStruct((height, keys), jnp.bfloat16),
            jax.ShapeDtypeStruct((height, keys), jnp.float32),
        ],
        scratch_shapes=[
            pltpu.VMEM((window // 8, keys), jnp.float32),
            pltpu.VMEM((window, keys), jnp.float32),
            pltpu.VMEM((window, keys), jnp.bfloat16),
            pltpu.VMEM((window, keys), jnp.bfloat16),
        ],
        compiler_params=pltpu.CompilerParams(vmem_limit_bytes=24 * 2**20),
        cost_estimate=pl.CostEstimate(
            flops=6 * height * window * keys, bytes_accessed=6_000_000, transcendentals=0
        ),
    )(got, left_basis, master_weight)


def shards(master_weight, gradient, first_moment, second_moment, left_basis, right_basis):
    own, cols = first_moment.shape
    depth = lax.axis_size("z")
    peers = lax.axis_size("y")
    few = own // 2
    keys = gradient.shape[1]
    xl, core, xh = lax.axis_index("xl"), lax.axis_index("core"), lax.axis_index("xh")
    correction = 1.0 - 0.95**STEP

    def trade(x, axis):
        mine = lax.dynamic_index_in_dim(x, xh, axis, keepdims=False)
        other = lax.dynamic_index_in_dim(x, 1 - xh, axis, keepdims=False)
        return mine, swap(other, "xh")

    by_xl = swap(right_basis, "xl")
    by_both = cross(right_basis)
    by_xh = relay(jnp.where(core == 0, by_both, by_xl))
    early = [x for ring in (right_basis, by_xl, by_both) for x in (ring, swap(ring, "core"))]

    parts = start(left_basis, gradient, peers)
    parts = exchange(parts.reshape((-1,) + parts.shape[3:]), ("xl", "core", "xh", "y"))
    parts, by_xh, early = lax.optimization_barrier((parts, by_xh, early))
    left_chunk = jnp.sum(parts.reshape(2, 2, 2 * peers, -1, LANES), axis=2)
    left_chunk = jnp.where(xl == 0, left_chunk, left_chunk[::-1])
    left_chunk = jnp.where(core == 0, left_chunk, left_chunk[:, ::-1])
    left_rotated = copies_to(left_chunk.reshape(-1, LANES), "y")
    basis = early[:4] + [by_xh, swap(by_xh, "core")] + early[4:]

    rotated = jnp.sum(exchange(forth(left_rotated, basis, few), "z"), axis=0)

    moments = jnp.stack([first_moment, second_moment]).reshape(2, 2, few, cols)
    moments = jnp.concatenate(trade(moments, 1), axis=1)
    new_first = 0.95 * moments[0] + 0.05 * rotated
    new_second = 0.95 * moments[1] + 0.05 * rotated * rotated
    normed = new_first / correction / (jnp.sqrt(new_second / correction) + 1e-08)

    column = lax.all_gather(normed, "z", axis=0, tiled=False)
    moments = jnp.stack([new_first, new_second]).reshape(2, 2, few, cols)
    mine, other = moments[:, 0], swap(moments[:, 1], "xh")
    moments = jnp.where(
        xh == 0, jnp.concatenate([mine, other], axis=1), jnp.concatenate([other, mine], axis=1)
    )

    me = (2 * xl + core).astype(jnp.int32).reshape(1)
    back_part = rotate_back(me, column, basis, peers)
    back_part = exchange(back_part.reshape((-1,) + back_part.shape[2:]), ("xl", "core", "y"))
    back_chunk = jnp.sum(back_part.reshape((4, peers) + back_part.shape[1:]), axis=1)
    got = copies_to(back_chunk, COL).reshape((2, peers) + back_chunk.shape)
    new_weight, direction = finish(got, left_basis, master_weight)
    return (new_weight, direction, moments[0], moments[1])


def solution(mesh):
    fine = Mesh(mesh.devices.reshape(12, 2, 2, 2, 8), ROW + COL)
    in_specs = (P(COL, ROW), P(COL, ROW), P(ROW, COL), P(ROW, COL), P(COL, None), P(ROW, COL))
    out_specs = (P(COL, ROW), P(COL, ROW), P(ROW, COL), P(ROW, COL))
    return jax.shard_map(shards, mesh=fine, in_specs=in_specs, out_specs=out_specs, check_vma=False)
```

```python
import jax
import jax.numpy as jnp
from jax import lax
from jax.experimental import pallas as pl
from jax.experimental.pallas import tpu as pltpu
from jax.sharding import Mesh, PartitionSpec as P

STEP = 10
LANES = 128
ROW = ("z", "xl", "core")
COL = ("xh", "y")


def swap(x, axis):
    return lax.ppermute(x, axis, [(0, 1), (1, 0)])


def cross(x, to_core=0):
    flip = 5 + 2 * to_core
    return lax.ppermute(x, ("xl", "core", "xh"), [(i, i ^ flip) for i in range(8)])


def exchange(x, axes):
    return lax.all_to_all(x, axes, 0, 0, tiled=True)


def copies_to(x, axes):
    return exchange(jnp.broadcast_to(x[None], (lax.axis_size(axes),) + x.shape), axes)


def split(x):
    high = x.astype(jnp.bfloat16)
    return high, (x - high.astype(jnp.float32)).astype(jnp.bfloat16)


def three_passes(a, b, contract):
    a_high, a_low = a
    b_high, b_low = b

    def one(x, y):
        return lax.dot_general(x, y, (contract, ((), ())), preferred_element_type=jnp.float32)

    return one(a_high, b_high) + (one(a_high, b_low) + one(a_low, b_high))


def start_kernel(left_ref, gradient_ref, out_ref, total, rows):
    step = pl.program_id(0)
    high, low = split(left_ref[...])
    turned = gradient_ref[...].astype(jnp.float32).T.astype(jnp.bfloat16)

    def one(x):
        return jnp.dot(turned, x, preferred_element_type=jnp.float32)

    part = one(high) + one(low)

    @pl.when(step == 0)
    def _():
        total[...] = part

    @pl.when(step > 0)
    def _():
        total[...] += part

    @pl.when(step == pl.num_programs(0) - 1)
    def _():
        whole = total[...].T
        peers, piece, few = out_ref.shape[2], out_ref.shape[3] // 2, 8
        for ring in range(4):
            for xh in range(2):
                for z in range(total.shape[1] // 64):
                    at = 64 * z + 16 * ring + few * xh
                    rows[few * z : few * (z + 1), :] = whole[at : at + few, :]
                for y in range(peers):
                    for part_of in range(2):
                        out_ref[ring, xh, y, piece * part_of : piece * (part_of + 1), :] = rows[
                            piece * y : piece * (y + 1), LANES * part_of : LANES * (part_of + 1)
                        ]


def start(left_basis, gradient, peers):
    height, window = left_basis.shape
    keys = gradient.shape[1]
    block = height // 3
    shape = (4, 2, peers, window // 8 // peers * (keys // LANES), LANES)
    return pl.pallas_call(
        start_kernel,
        grid=(3,),
        in_specs=[
            pl.BlockSpec((block, window), lambda i: (i, 0)),
            pl.BlockSpec((block, keys), lambda i: (i, 0)),
        ],
        out_specs=pl.BlockSpec(shape, lambda i: (0,) * 5),
        out_shape=jax.ShapeDtypeStruct(shape, jnp.float32),
        scratch_shapes=[
            pltpu.VMEM((keys, window), jnp.float32),
            pltpu.VMEM((window // 8, keys), jnp.float32),
        ],
        compiler_params=pltpu.CompilerParams(vmem_limit_bytes=59 * 2**20),
        cost_estimate=pl.CostEstimate(
            flops=4 * height * window * keys, bytes_accessed=4_000_000, transcendentals=0
        ),
    )(left_basis, gradient)


def forth_kernel(left_ref, *refs):
    basis, (out_ref, rows, high, low) = refs[:8], refs[8:]
    keys = basis[0].shape[0]

    @pl.when(pl.program_id(0) == 0)
    def _():
        peers, tiles = left_ref.shape[0], rows.shape[1] // LANES
        piece = left_ref.shape[1] // tiles
        for y in range(peers):
            for tile in range(tiles):
                rows[piece * y : piece * (y + 1), LANES * tile : LANES * (tile + 1)] = left_ref[
                    y, piece * tile : piece * (tile + 1), :
                ]
        high[...], low[...] = split(rows[...])

    few = out_ref.shape[1] // 2
    for half in range(2):
        total = None
        for i in range(4):
            at = slice(keys * i, keys * (i + 1))
            term = three_passes(
                (high[:, at], low[:, at]), split(basis[4 * half + i][...]), ((1,), (0,))
            )
            total = term if total is None else total + term
        out_ref[:, few * half : few * (half + 1), :] = total.reshape(-1, few, total.shape[1])


def forth(left, basis, few):
    keys, cols = basis[0].shape
    count = left.shape[0] * left.shape[1] * LANES // (4 * keys)
    block = cols // 3
    depth = count // few
    return pl.pallas_call(
        forth_kernel,
        grid=(3,),
        in_specs=[pl.BlockSpec(left.shape, lambda j: (0, 0, 0))]
        + [pl.BlockSpec((keys, block), lambda j: (0, j))] * 8,
        out_specs=pl.BlockSpec((depth, 2 * few, block), lambda j: (0, 0, j)),
        out_shape=pltpu.HBM((depth, 2 * few, cols), jnp.float32),
        scratch_shapes=[
            pltpu.VMEM((count, 4 * keys), jnp.float32),
            pltpu.VMEM((count, 4 * keys), jnp.bfloat16),
            pltpu.VMEM((count, 4 * keys), jnp.bfloat16),
        ],
        compiler_params=pltpu.CompilerParams(vmem_limit_bytes=24 * 2**20),
        cost_estimate=pl.CostEstimate(
            flops=48 * count * keys * cols, bytes_accessed=8_000_000, transcendentals=0
        ),
    )(left, *basis)


def back_kernel(me_ref, column_ref, *refs):
    basis, (out_ref, rows, whole, high, low) = refs[:8], refs[8:]
    few = column_ref.shape[1] // 2
    step = pl.program_id(0)

    @pl.when(step == 0)
    def _():
        for half in range(2):
            for z in range(column_ref.shape[0]):
                whole[half, few * z : few * (z + 1), :] = column_ref[
                    z, few * half : few * (half + 1), :
                ]
        high[...], low[...] = split(whole[...])

    peers, piece = out_ref.shape[1], out_ref.shape[2] // 2
    for i in range(4):
        first, second = (
            three_passes((high[half], low[half]), split(basis[4 * half + i][...]), ((1,), (1,)))
            for half in range(2)
        )
        rows[i] = first + second
    for part in range(2):

        @pl.when(step == part)
        def _():
            for i in range(4):
                ring = jnp.bitwise_xor(me_ref[0], i)
                for y in range(peers):
                    out_ref[ring, y, piece * part : piece * (part + 1), :] = rows[
                        i, piece * y : piece * (y + 1), :
                    ]


def rotate_back(me, column, basis, peers):
    keys, cols = basis[0].shape
    depth, both, _ = column.shape
    count = depth * both // 2
    shape = (4, peers, 2 * count // peers, LANES)
    return pl.pallas_call(
        back_kernel,
        grid=(2,),
        in_specs=[
            pl.BlockSpec(memory_space=pltpu.SMEM),
            pl.BlockSpec(column.shape, lambda i: (0, 0, 0)),
        ]
        + [pl.BlockSpec((LANES, cols), lambda i: (i, 0))] * 8,
        out_specs=pl.BlockSpec(shape, lambda i: (0, 0, 0, 0)),
        out_shape=jax.ShapeDtypeStruct(shape, jnp.float32),
        scratch_shapes=[
            pltpu.VMEM((4, count, LANES), jnp.float32),
            pltpu.VMEM((2, count, cols), jnp.float32),
            pltpu.VMEM((2, count, cols), jnp.bfloat16),
            pltpu.VMEM((2, count, cols), jnp.bfloat16),
        ],
        compiler_params=pltpu.CompilerParams(vmem_limit_bytes=24 * 2**20),
        cost_estimate=pl.CostEstimate(
            flops=48 * count * keys * cols, bytes_accessed=8_000_000, transcendentals=0
        ),
    )(me, column, *basis)


def finish_kernel(got_ref, left_ref, master_ref, weight_ref, direction_ref, rows, back, high, low):
    peers, few = got_ref.shape[1], 8
    piece = got_ref.shape[3] // 2
    depth = back.shape[0] // 64

    @pl.when(pl.program_id(0) == 0)
    def _():
        for xh in range(2):
            for ring in range(4):
                for y in range(peers):
                    for part in range(2):
                        rows[piece * y : piece * (y + 1), LANES * part : LANES * (part + 1)] = got_ref[
                            xh, y, ring, piece * part : piece * (part + 1), :
                        ]
                for z in range(depth):
                    at = 64 * z + 16 * ring + few * xh
                    back[at : at + few, :] = rows[few * z : few * (z + 1), :]
        high[...], low[...] = split(back[...])

    step = three_passes(split(left_ref[...]), (high[...], low[...]), ((1,), (0,)))
    master = master_ref[...]
    direction_ref[...] = step
    weight_ref[...] = (master - 0.003 * (step + 0.1 * master)).astype(jnp.bfloat16)


def finish(got, left_basis, master_weight):
    height, keys = master_weight.shape
    window = left_basis.shape[1]
    block = height // 4
    by_rows = pl.BlockSpec((block, keys), lambda i: (i, 0))
    return pl.pallas_call(
        finish_kernel,
        grid=(4,),
        in_specs=[
            pl.BlockSpec(got.shape, lambda i: (0,) * got.ndim),
            pl.BlockSpec((block, window), lambda i: (i, 0)),
            by_rows,
        ],
        out_specs=[by_rows, by_rows],
        out_shape=[
            jax.ShapeDtypeStruct((height, keys), jnp.bfloat16),
            jax.ShapeDtypeStruct((height, keys), jnp.float32),
        ],
        scratch_shapes=[
            pltpu.VMEM((window // 8, keys), jnp.float32),
            pltpu.VMEM((window, keys), jnp.float32),
            pltpu.VMEM((window, keys), jnp.bfloat16),
            pltpu.VMEM((window, keys), jnp.bfloat16),
        ],
        compiler_params=pltpu.CompilerParams(vmem_limit_bytes=24 * 2**20),
        cost_estimate=pl.CostEstimate(
            flops=6 * height * window * keys, bytes_accessed=6_000_000, transcendentals=0
        ),
    )(got, left_basis, master_weight)


def shards(master_weight, gradient, first_moment, second_moment, left_basis, right_basis):
    own, cols = first_moment.shape
    depth = lax.axis_size("z")
    peers = lax.axis_size("y")
    few = own // 2
    keys = gradient.shape[1]
    xl, core, xh = lax.axis_index("xl"), lax.axis_index("core"), lax.axis_index("xh")
    correction = 1.0 - 0.95**STEP

    def trade(x, axis):
        mine = lax.dynamic_index_in_dim(x, xh, axis, keepdims=False)
        other = lax.dynamic_index_in_dim(x, 1 - xh, axis, keepdims=False)
        return mine, swap(other, "xh")

    by_xl, by_both = swap(right_basis, "xl"), cross(right_basis)
    by_xh, by_xh_core = swap(by_both, "xl"), cross(by_xl, to_core=1)
    early = [x for ring in (right_basis, by_xl, by_both) for x in (ring, swap(ring, "core"))]

    parts = start(left_basis, gradient, peers)
    parts = exchange(parts.reshape((-1,) + parts.shape[3:]), ("xl", "core", "xh", "y"))
    parts, early = lax.optimization_barrier((parts, early))
    left_chunk = jnp.sum(parts.reshape(2, 2, 2 * peers, -1, LANES), axis=2)
    left_chunk = jnp.where(xl == 0, left_chunk, left_chunk[::-1])
    left_chunk = jnp.where(core == 0, left_chunk, left_chunk[:, ::-1])
    left_rotated = copies_to(left_chunk.reshape(-1, LANES), "y")
    basis = early[:4] + [by_xh, by_xh_core] + early[4:]

    rotated = jnp.sum(exchange(forth(left_rotated, basis, few), "z"), axis=0)

    moments = jnp.stack([first_moment, second_moment]).reshape(2, 2, few, cols)
    moments = jnp.concatenate(trade(moments, 1), axis=1)
    new_first = 0.95 * moments[0] + 0.05 * rotated
    new_second = 0.95 * moments[1] + 0.05 * rotated * rotated
    normed = new_first / correction / (jnp.sqrt(new_second / correction) + 1e-08)

    column = lax.all_gather(normed, "z", axis=0, tiled=False)
    moments = jnp.stack([new_first, new_second]).reshape(2, 2, few, cols)
    mine, other = moments[:, 0], swap(moments[:, 1], "xh")
    moments = jnp.where(
        xh == 0, jnp.concatenate([mine, other], axis=1), jnp.concatenate([other, mine], axis=1)
    )

    me = (2 * xl + core).astype(jnp.int32).reshape(1)
    back_part = rotate_back(me, column, basis, peers)
    back_part = exchange(back_part.reshape((-1,) + back_part.shape[2:]), ("xl", "core", "y"))
    back_chunk = jnp.sum(back_part.reshape((4, peers) + back_part.shape[1:]), axis=1)
    got = copies_to(back_chunk, COL).reshape((2, peers) + back_chunk.shape)
    new_weight, direction = finish(got, left_basis, master_weight)
    return (new_weight, direction, moments[0], moments[1])


def solution(mesh):
    fine = Mesh(mesh.devices.reshape(12, 2, 2, 2, 8), ROW + COL)
    in_specs = (P(COL, ROW), P(COL, ROW), P(ROW, COL), P(ROW, COL), P(COL, None), P(ROW, COL))
    out_specs = (P(COL, ROW), P(COL, ROW), P(ROW, COL), P(ROW, COL))
    return jax.shard_map(shards, mesh=fine, in_specs=in_specs, out_specs=out_specs, check_vma=False)
```

```python
import jax
import jax.numpy as jnp
from jax import lax
from jax.experimental import pallas as pl
from jax.experimental.pallas import tpu as pltpu
from jax.sharding import Mesh, PartitionSpec as P

STEP = 10
LANES = 128
ROW = ("z", "xl", "core")
COL = ("xh", "y")


def swap(x, axis):
    return lax.ppermute(x, axis, [(0, 1), (1, 0)])


def cross(x, to_core=0):
    flip = 5 + 2 * to_core
    return lax.ppermute(x, ("xl", "core", "xh"), [(i, i ^ flip) for i in range(8)])


def exchange(x, axes):
    return lax.all_to_all(x, axes, 0, 0, tiled=True)


def copies_to(x, axes):
    return exchange(jnp.broadcast_to(x[None], (lax.axis_size(axes),) + x.shape), axes)


def split(x):
    high = x.astype(jnp.bfloat16)
    return high, (x - high.astype(jnp.float32)).astype(jnp.bfloat16)


def three_passes(a, b, contract):
    a_high, a_low = a
    b_high, b_low = b

    def one(x, y):
        return lax.dot_general(x, y, (contract, ((), ())), preferred_element_type=jnp.float32)

    return one(a_high, b_high) + (one(a_high, b_low) + one(a_low, b_high))


def start_kernel(left_ref, gradient_ref, out_ref, total, rows):
    step = pl.program_id(0)
    high, low = split(left_ref[...])
    turned = gradient_ref[...].astype(jnp.float32).T.astype(jnp.bfloat16)

    def one(x):
        return jnp.dot(turned, x, preferred_element_type=jnp.float32)

    part = one(high) + one(low)

    @pl.when(step == 0)
    def _():
        total[...] = part

    @pl.when(step > 0)
    def _():
        total[...] += part

    @pl.when(step == pl.num_programs(0) - 1)
    def _():
        whole = total[...].T
        peers, piece, few = out_ref.shape[2], out_ref.shape[3] // 2, 8
        for ring in range(4):
            for xh in range(2):
                for z in range(total.shape[1] // 64):
                    at = 64 * z + 16 * ring + few * xh
                    rows[few * z : few * (z + 1), :] = whole[at : at + few, :]
                for y in range(peers):
                    for part_of in range(2):
                        out_ref[ring, xh, y, piece * part_of : piece * (part_of + 1), :] = rows[
                            piece * y : piece * (y + 1), LANES * part_of : LANES * (part_of + 1)
                        ]


def start(left_basis, gradient, peers):
    height, window = left_basis.shape
    keys = gradient.shape[1]
    block = height // 3
    shape = (4, 2, peers, window // 8 // peers * (keys // LANES), LANES)
    return pl.pallas_call(
        start_kernel,
        grid=(3,),
        in_specs=[
            pl.BlockSpec((block, window), lambda i: (i, 0)),
            pl.BlockSpec((block, keys), lambda i: (i, 0)),
        ],
        out_specs=pl.BlockSpec(shape, lambda i: (0,) * 5),
        out_shape=jax.ShapeDtypeStruct(shape, jnp.float32),
        scratch_shapes=[
            pltpu.VMEM((keys, window), jnp.float32),
            pltpu.VMEM((window // 8, keys), jnp.float32),
        ],
        compiler_params=pltpu.CompilerParams(vmem_limit_bytes=59 * 2**20),
        cost_estimate=pl.CostEstimate(
            flops=4 * height * window * keys, bytes_accessed=4_000_000, transcendentals=0
        ),
    )(left_basis, gradient)


def forth_kernel(left_ref, *refs):
    basis, (out_ref, rows, high, low) = refs[:8], refs[8:]
    keys = basis[0].shape[0]

    @pl.when(pl.program_id(0) == 0)
    def _():
        peers, tiles = left_ref.shape[0], rows.shape[1] // LANES
        piece = left_ref.shape[1] // tiles
        for y in range(peers):
            for tile in range(tiles):
                rows[piece * y : piece * (y + 1), LANES * tile : LANES * (tile + 1)] = left_ref[
                    y, piece * tile : piece * (tile + 1), :
                ]
        high[...], low[...] = split(rows[...])

    few = out_ref.shape[1] // 2
    for half in range(2):
        total = None
        for i in range(4):
            at = slice(keys * i, keys * (i + 1))
            term = three_passes(
                (high[:, at], low[:, at]), split(basis[4 * half + i][...]), ((1,), (0,))
            )
            total = term if total is None else total + term
        out_ref[:, few * half : few * (half + 1), :] = total.reshape(-1, few, total.shape[1])


def forth(left, basis, few):
    keys, cols = basis[0].shape
    count = left.shape[0] * left.shape[1] * LANES // (4 * keys)
    block = cols // 3
    depth = count // few
    return pl.pallas_call(
        forth_kernel,
        grid=(3,),
        in_specs=[pl.BlockSpec(left.shape, lambda j: (0, 0, 0))]
        + [pl.BlockSpec((keys, block), lambda j: (0, j))] * 8,
        out_specs=pl.BlockSpec((depth, 2 * few, block), lambda j: (0, 0, j)),
        out_shape=pltpu.HBM((depth, 2 * few, cols), jnp.float32),
        scratch_shapes=[
            pltpu.VMEM((count, 4 * keys), jnp.float32),
            pltpu.VMEM((count, 4 * keys), jnp.bfloat16),
            pltpu.VMEM((count, 4 * keys), jnp.bfloat16),
        ],
        compiler_params=pltpu.CompilerParams(vmem_limit_bytes=24 * 2**20),
        cost_estimate=pl.CostEstimate(
            flops=48 * count * keys * cols, bytes_accessed=8_000_000, transcendentals=0
        ),
    )(left, *basis)


def back_kernel(me_ref, column_ref, *refs):
    basis, (out_ref, rows, whole, high, low) = refs[:8], refs[8:]
    few = column_ref.shape[1] // 2
    step = pl.program_id(0)

    @pl.when(step == 0)
    def _():
        for half in range(2):
            for z in range(column_ref.shape[0]):
                whole[half, few * z : few * (z + 1), :] = column_ref[
                    z, few * half : few * (half + 1), :
                ]
        high[...], low[...] = split(whole[...])

    peers, piece = out_ref.shape[1], out_ref.shape[2] // 2
    for i in range(4):
        first, second = (
            three_passes((high[half], low[half]), split(basis[4 * half + i][...]), ((1,), (1,)))
            for half in range(2)
        )
        rows[i] = first + second
    for part in range(2):

        @pl.when(step == part)
        def _():
            for i in range(4):
                ring = jnp.bitwise_xor(me_ref[0], i)
                for y in range(peers):
                    out_ref[ring, y, piece * part : piece * (part + 1), :] = rows[
                        i, piece * y : piece * (y + 1), :
                    ]


def rotate_back(me, column, basis, peers):
    keys, cols = basis[0].shape
    depth, both, _ = column.shape
    count = depth * both // 2
    shape = (4, peers, 2 * count // peers, LANES)
    return pl.pallas_call(
        back_kernel,
        grid=(2,),
        in_specs=[
            pl.BlockSpec(memory_space=pltpu.SMEM),
            pl.BlockSpec(column.shape, lambda i: (0, 0, 0)),
        ]
        + [pl.BlockSpec((LANES, cols), lambda i: (i, 0))] * 8,
        out_specs=pl.BlockSpec(shape, lambda i: (0, 0, 0, 0)),
        out_shape=jax.ShapeDtypeStruct(shape, jnp.float32),
        scratch_shapes=[
            pltpu.VMEM((4, count, LANES), jnp.float32),
            pltpu.VMEM((2, count, cols), jnp.float32),
            pltpu.VMEM((2, count, cols), jnp.bfloat16),
            pltpu.VMEM((2, count, cols), jnp.bfloat16),
        ],
        compiler_params=pltpu.CompilerParams(vmem_limit_bytes=24 * 2**20),
        cost_estimate=pl.CostEstimate(
            flops=48 * count * keys * cols, bytes_accessed=8_000_000, transcendentals=0
        ),
    )(me, column, *basis)


def finish_kernel(got_ref, left_ref, master_ref, weight_ref, direction_ref, rows, back, high, low):
    peers, few = got_ref.shape[1], 8
    piece = got_ref.shape[3] // 2
    depth = back.shape[0] // 64

    @pl.when(pl.program_id(0) == 0)
    def _():
        for xh in range(2):
            for ring in range(4):
                for y in range(peers):
                    for part in range(2):
                        rows[piece * y : piece * (y + 1), LANES * part : LANES * (part + 1)] = got_ref[
                            xh, y, ring, piece * part : piece * (part + 1), :
                        ]
                for z in range(depth):
                    at = 64 * z + 16 * ring + few * xh
                    back[at : at + few, :] = rows[few * z : few * (z + 1), :]
        high[...], low[...] = split(back[...])

    step = three_passes(split(left_ref[...]), (high[...], low[...]), ((1,), (0,)))
    master = master_ref[...]
    direction_ref[...] = step
    weight_ref[...] = (master - 0.003 * (step + 0.1 * master)).astype(jnp.bfloat16)


def finish(got, left_basis, master_weight):
    height, keys = master_weight.shape
    window = left_basis.shape[1]
    block = height // 4
    by_rows = pl.BlockSpec((block, keys), lambda i: (i, 0))
    return pl.pallas_call(
        finish_kernel,
        grid=(4,),
        in_specs=[
            pl.BlockSpec(got.shape, lambda i: (0,) * got.ndim),
            pl.BlockSpec((block, window), lambda i: (i, 0)),
            by_rows,
        ],
        out_specs=[by_rows, by_rows],
        out_shape=[
            jax.ShapeDtypeStruct((height, keys), jnp.bfloat16),
            jax.ShapeDtypeStruct((height, keys), jnp.float32),
        ],
        scratch_shapes=[
            pltpu.VMEM((window // 8, keys), jnp.float32),
            pltpu.VMEM((window, keys), jnp.float32),
            pltpu.VMEM((window, keys), jnp.bfloat16),
            pltpu.VMEM((window, keys), jnp.bfloat16),
        ],
        compiler_params=pltpu.CompilerParams(vmem_limit_bytes=24 * 2**20),
        cost_estimate=pl.CostEstimate(
            flops=6 * height * window * keys, bytes_accessed=6_000_000, transcendentals=0
        ),
    )(got, left_basis, master_weight)


def shards(master_weight, gradient, first_moment, second_moment, left_basis, right_basis):
    own, cols = first_moment.shape
    depth = lax.axis_size("z")
    peers = lax.axis_size("y")
    few = own // 2
    keys = gradient.shape[1]
    xl, core, xh = lax.axis_index("xl"), lax.axis_index("core"), lax.axis_index("xh")
    correction = 1.0 - 0.95**STEP

    def trade(x, axis):
        mine = lax.dynamic_index_in_dim(x, xh, axis, keepdims=False)
        other = lax.dynamic_index_in_dim(x, 1 - xh, axis, keepdims=False)
        return mine, swap(other, "xh")

    by_xl, by_both = swap(right_basis, "xl"), cross(right_basis)
    by_xh, by_xh_core = swap(by_both, "xl"), cross(by_xl, to_core=1)
    early = [x for ring in (right_basis, by_xl, by_both) for x in (ring, swap(ring, "core"))]

    parts = start(left_basis, gradient, peers)
    parts = exchange(parts.reshape((-1,) + parts.shape[3:]), ("xl", "core", "xh", "y"))
    parts, early = lax.optimization_barrier((parts, early))
    left_chunk = jnp.sum(parts.reshape(2, 2, 2 * peers, -1, LANES), axis=2)
    left_chunk = jnp.where(xl == 0, left_chunk, left_chunk[::-1])
    left_chunk = jnp.where(core == 0, left_chunk, left_chunk[:, ::-1])
    left_rotated = copies_to(left_chunk.reshape(-1, LANES), "y")
    basis = early[:4] + [by_xh, by_xh_core] + early[4:]

    rotated = jnp.sum(exchange(forth(left_rotated, basis, few), "z"), axis=0)

    moments = jnp.stack([first_moment, second_moment]).reshape(2, 2, few, cols)
    moments = jnp.concatenate(trade(moments, 1), axis=1)
    new_first = 0.95 * moments[0] + 0.05 * rotated
    new_second = 0.95 * moments[1] + 0.05 * rotated * rotated
    normed = new_first / correction / (jnp.sqrt(new_second / correction) + 1e-08)

    column = lax.all_gather(normed, "z", axis=0, tiled=False)
    moments = jnp.stack([new_first, new_second]).reshape(2, 2, few, cols)
    mine, other = moments[:, 0], swap(moments[:, 1], "xh")
    moments = jnp.where(
        xh == 0, jnp.concatenate([mine, other], axis=1), jnp.concatenate([other, mine], axis=1)
    )

    me = (2 * xl + core).astype(jnp.int32).reshape(1)
    back_part = rotate_back(me, column, basis, peers)
    back_part = exchange(back_part.reshape((-1,) + back_part.shape[2:]), ("xl", "core", "y"))
    back_part, *moments = lax.optimization_barrier((back_part, moments[0], moments[1]))
    back_chunk = jnp.sum(back_part.reshape((4, peers) + back_part.shape[1:]), axis=1)
    got = copies_to(back_chunk, COL).reshape((2, peers) + back_chunk.shape)
    new_weight, direction = finish(got, left_basis, master_weight)
    return (new_weight, direction, moments[0], moments[1])


def solution(mesh):
    fine = Mesh(mesh.devices.reshape(12, 2, 2, 2, 8), ROW + COL)
    in_specs = (P(COL, ROW), P(COL, ROW), P(ROW, COL), P(ROW, COL), P(COL, None), P(ROW, COL))
    out_specs = (P(COL, ROW), P(COL, ROW), P(ROW, COL), P(ROW, COL))
    return jax.shard_map(shards, mesh=fine, in_specs=in_specs, out_specs=out_specs, check_vma=False)
```

```python
import jax
import jax.numpy as jnp
from jax import lax
from jax.experimental import pallas as pl
from jax.experimental.pallas import tpu as pltpu
from jax.sharding import Mesh, PartitionSpec as P

STEP = 10
LANES = 128
ROW = ("z", "xl", "core")
COL = ("xh", "y")


def swap(x, axis):
    return lax.ppermute(x, axis, [(0, 1), (1, 0)])


def cross(x, to_core=0):
    flip = 5 + 2 * to_core
    return lax.ppermute(x, ("xl", "core", "xh"), [(i, i ^ flip) for i in range(8)])


def exchange(x, axes):
    return lax.all_to_all(x, axes, 0, 0, tiled=True)


def copies_to(x, axes):
    return exchange(jnp.broadcast_to(x[None], (lax.axis_size(axes),) + x.shape), axes)


def split(x):
    high = x.astype(jnp.bfloat16)
    return high, (x - high.astype(jnp.float32)).astype(jnp.bfloat16)


def three_passes(a, b, contract):
    a_high, a_low = a
    b_high, b_low = b

    def one(x, y):
        return lax.dot_general(x, y, (contract, ((), ())), preferred_element_type=jnp.float32)

    return one(a_high, b_high) + (one(a_high, b_low) + one(a_low, b_high))


def start_kernel(left_ref, gradient_ref, out_ref, total, rows):
    step = pl.program_id(0)
    high, low = split(left_ref[...])
    turned = gradient_ref[...].astype(jnp.float32).T.astype(jnp.bfloat16)

    def one(x):
        return jnp.dot(turned, x, preferred_element_type=jnp.float32)

    part = one(high) + one(low)

    @pl.when(step == 0)
    def _():
        total[...] = part

    @pl.when(step > 0)
    def _():
        total[...] += part

    @pl.when(step == pl.num_programs(0) - 1)
    def _():
        whole = total[...].T
        peers, piece, few = out_ref.shape[2], out_ref.shape[3] // 2, 8
        for ring in range(4):
            for xh in range(2):
                for z in range(total.shape[1] // 64):
                    at = 64 * z + 16 * ring + few * xh
                    rows[few * z : few * (z + 1), :] = whole[at : at + few, :]
                for y in range(peers):
                    for part_of in range(2):
                        out_ref[ring, xh, y, piece * part_of : piece * (part_of + 1), :] = rows[
                            piece * y : piece * (y + 1), LANES * part_of : LANES * (part_of + 1)
                        ]


def start(left_basis, gradient, peers):
    height, window = left_basis.shape
    keys = gradient.shape[1]
    block = height // 3
    shape = (4, 2, peers, window // 8 // peers * (keys // LANES), LANES)
    return pl.pallas_call(
        start_kernel,
        grid=(3,),
        in_specs=[
            pl.BlockSpec((block, window), lambda i: (i, 0)),
            pl.BlockSpec((block, keys), lambda i: (i, 0)),
        ],
        out_specs=pl.BlockSpec(shape, lambda i: (0,) * 5),
        out_shape=jax.ShapeDtypeStruct(shape, jnp.float32),
        scratch_shapes=[
            pltpu.VMEM((keys, window), jnp.float32),
            pltpu.VMEM((window // 8, keys), jnp.float32),
        ],
        compiler_params=pltpu.CompilerParams(vmem_limit_bytes=59 * 2**20),
        cost_estimate=pl.CostEstimate(
            flops=4 * height * window * keys, bytes_accessed=4_000_000, transcendentals=0
        ),
    )(left_basis, gradient)


def forth_kernel(left_ref, *refs):
    basis, (out_ref, rows, high, low) = refs[:8], refs[8:]
    keys = basis[0].shape[0]

    @pl.when(pl.program_id(0) == 0)
    def _():
        peers, tiles = left_ref.shape[0], rows.shape[1] // LANES
        piece = left_ref.shape[1] // tiles
        for y in range(peers):
            for tile in range(tiles):
                rows[piece * y : piece * (y + 1), LANES * tile : LANES * (tile + 1)] = left_ref[
                    y, piece * tile : piece * (tile + 1), :
                ]
        high[...], low[...] = split(rows[...])

    few = out_ref.shape[1] // 2
    for half in range(2):
        total = None
        for i in range(4):
            at = slice(keys * i, keys * (i + 1))
            term = three_passes(
                (high[:, at], low[:, at]), split(basis[4 * half + i][...]), ((1,), (0,))
            )
            total = term if total is None else total + term
        out_ref[:, few * half : few * (half + 1), :] = total.reshape(-1, few, total.shape[1])


def forth(left, basis, few):
    keys, cols = basis[0].shape
    count = left.shape[0] * left.shape[1] * LANES // (4 * keys)
    block = cols // 3
    depth = count // few
    return pl.pallas_call(
        forth_kernel,
        grid=(3,),
        in_specs=[pl.BlockSpec(left.shape, lambda j: (0, 0, 0))]
        + [pl.BlockSpec((keys, block), lambda j: (0, j))] * 8,
        out_specs=pl.BlockSpec((depth, 2 * few, block), lambda j: (0, 0, j)),
        out_shape=pltpu.HBM((depth, 2 * few, cols), jnp.float32),
        scratch_shapes=[
            pltpu.VMEM((count, 4 * keys), jnp.float32),
            pltpu.VMEM((count, 4 * keys), jnp.bfloat16),
            pltpu.VMEM((count, 4 * keys), jnp.bfloat16),
        ],
        compiler_params=pltpu.CompilerParams(vmem_limit_bytes=24 * 2**20),
        cost_estimate=pl.CostEstimate(
            flops=48 * count * keys * cols, bytes_accessed=8_000_000, transcendentals=0
        ),
    )(left, *basis)


def back_kernel(me_ref, column_ref, *refs):
    basis, (out_ref, rows, whole, high, low) = refs[:8], refs[8:]
    few = column_ref.shape[1] // 2
    step = pl.program_id(0)

    @pl.when(step == 0)
    def _():
        for half in range(2):
            for z in range(column_ref.shape[0]):
                whole[half, few * z : few * (z + 1), :] = column_ref[
                    z, few * half : few * (half + 1), :
                ]
        high[...], low[...] = split(whole[...])

    peers, piece = out_ref.shape[1], out_ref.shape[2] // 2
    for i in range(4):
        first, second = (
            three_passes((high[half], low[half]), split(basis[4 * half + i][...]), ((1,), (1,)))
            for half in range(2)
        )
        rows[i] = first + second
    for part in range(2):

        @pl.when(step == part)
        def _():
            for i in range(4):
                ring = jnp.bitwise_xor(me_ref[0], i)
                for y in range(peers):
                    out_ref[ring, y, piece * part : piece * (part + 1), :] = rows[
                        i, piece * y : piece * (y + 1), :
                    ]


def rotate_back(me, column, basis, peers):
    keys, cols = basis[0].shape
    depth, both, _ = column.shape
    count = depth * both // 2
    shape = (4, peers, 2 * count // peers, LANES)
    return pl.pallas_call(
        back_kernel,
        grid=(2,),
        in_specs=[
            pl.BlockSpec(memory_space=pltpu.SMEM),
            pl.BlockSpec(column.shape, lambda i: (0, 0, 0)),
        ]
        + [pl.BlockSpec((LANES, cols), lambda i: (i, 0))] * 8,
        out_specs=pl.BlockSpec(shape, lambda i: (0, 0, 0, 0)),
        out_shape=jax.ShapeDtypeStruct(shape, jnp.float32),
        scratch_shapes=[
            pltpu.VMEM((4, count, LANES), jnp.float32),
            pltpu.VMEM((2, count, cols), jnp.float32),
            pltpu.VMEM((2, count, cols), jnp.bfloat16),
            pltpu.VMEM((2, count, cols), jnp.bfloat16),
        ],
        compiler_params=pltpu.CompilerParams(vmem_limit_bytes=24 * 2**20),
        cost_estimate=pl.CostEstimate(
            flops=48 * count * keys * cols, bytes_accessed=8_000_000, transcendentals=0
        ),
    )(me, column, *basis)


def sum_kernel(me_ref, parts_ref, out_ref):
    for i in range(parts_ref.shape[0]):
        total = jnp.sum(parts_ref[jnp.bitwise_xor(me_ref[0], i)], axis=0)
        for peer in range(out_ref.shape[0]):
            out_ref[peer, i] = total


def sum_and_copy(me, parts, peers):
    ring, senders, *block = parts.shape
    shape = (peers, ring, *block)
    return pl.pallas_call(
        sum_kernel,
        grid=(1,),
        in_specs=[
            pl.BlockSpec(memory_space=pltpu.SMEM),
            pl.BlockSpec(parts.shape, lambda i: (0, 0, 0, 0)),
        ],
        out_specs=pl.BlockSpec(shape, lambda i: (0, 0, 0, 0)),
        out_shape=pltpu.HBM(shape, jnp.float32),
        compiler_params=pltpu.CompilerParams(vmem_limit_bytes=24 * 2**20),
        cost_estimate=pl.CostEstimate(
            flops=ring * senders * block[0] * LANES, bytes_accessed=1_200_000, transcendentals=0
        ),
    )(me, parts)


def finish_kernel(got_ref, left_ref, master_ref, weight_ref, direction_ref, rows, back, high, low):
    peers, few = got_ref.shape[1], 8
    piece = got_ref.shape[3] // 2
    depth = back.shape[0] // 64

    @pl.when(pl.program_id(0) == 0)
    def _():
        for xh in range(2):
            for ring in range(4):
                for y in range(peers):
                    for part in range(2):
                        rows[piece * y : piece * (y + 1), LANES * part : LANES * (part + 1)] = got_ref[
                            xh, y, ring, piece * part : piece * (part + 1), :
                        ]
                for z in range(depth):
                    at = 64 * z + 16 * ring + few * xh
                    back[at : at + few, :] = rows[few * z : few * (z + 1), :]
        high[...], low[...] = split(back[...])

    step = three_passes(split(left_ref[...]), (high[...], low[...]), ((1,), (0,)))
    master = master_ref[...]
    direction_ref[...] = step
    weight_ref[...] = (master - 0.003 * (step + 0.1 * master)).astype(jnp.bfloat16)


def finish(got, left_basis, master_weight):
    height, keys = master_weight.shape
    window = left_basis.shape[1]
    block = height // 4
    by_rows = pl.BlockSpec((block, keys), lambda i: (i, 0))
    return pl.pallas_call(
        finish_kernel,
        grid=(4,),
        in_specs=[
            pl.BlockSpec(got.shape, lambda i: (0,) * got.ndim),
            pl.BlockSpec((block, window), lambda i: (i, 0)),
            by_rows,
        ],
        out_specs=[by_rows, by_rows],
        out_shape=[
            jax.ShapeDtypeStruct((height, keys), jnp.bfloat16),
            jax.ShapeDtypeStruct((height, keys), jnp.float32),
        ],
        scratch_shapes=[
            pltpu.VMEM((window // 8, keys), jnp.float32),
            pltpu.VMEM((window, keys), jnp.float32),
            pltpu.VMEM((window, keys), jnp.bfloat16),
            pltpu.VMEM((window, keys), jnp.bfloat16),
        ],
        compiler_params=pltpu.CompilerParams(vmem_limit_bytes=24 * 2**20),
        cost_estimate=pl.CostEstimate(
            flops=6 * height * window * keys, bytes_accessed=6_000_000, transcendentals=0
        ),
    )(got, left_basis, master_weight)


def shards(master_weight, gradient, first_moment, second_moment, left_basis, right_basis):
    own, cols = first_moment.shape
    depth = lax.axis_size("z")
    peers = lax.axis_size("y")
    few = own // 2
    keys = gradient.shape[1]
    xl, core, xh = lax.axis_index("xl"), lax.axis_index("core"), lax.axis_index("xh")
    correction = 1.0 - 0.95**STEP

    def trade(x, axis):
        mine = lax.dynamic_index_in_dim(x, xh, axis, keepdims=False)
        other = lax.dynamic_index_in_dim(x, 1 - xh, axis, keepdims=False)
        return mine, swap(other, "xh")

    by_xl, by_both = swap(right_basis, "xl"), cross(right_basis)
    by_xh, by_xh_core = swap(by_both, "xl"), cross(by_xl, to_core=1)
    early = [x for ring in (right_basis, by_xl, by_both) for x in (ring, swap(ring, "core"))]

    parts = start(left_basis, gradient, peers)
    parts = exchange(parts.reshape((-1,) + parts.shape[3:]), ("xl", "core", "xh", "y"))
    parts, early = lax.optimization_barrier((parts, early))
    me = (2 * xl + core).astype(jnp.int32).reshape(1)
    left_copies = sum_and_copy(me, parts.reshape(4, 2 * peers, -1, LANES), peers)
    left_rotated = exchange(left_copies.reshape(peers, -1, LANES), "y")
    basis = early[:4] + [by_xh, by_xh_core] + early[4:]

    rotated = jnp.sum(exchange(forth(left_rotated, basis, few), "z"), axis=0)

    moments = jnp.stack([first_moment, second_moment]).reshape(2, 2, few, cols)
    moments = jnp.concatenate(trade(moments, 1), axis=1)
    new_first = 0.95 * moments[0] + 0.05 * rotated
    new_second = 0.95 * moments[1] + 0.05 * rotated * rotated
    normed = new_first / correction / (jnp.sqrt(new_second / correction) + 1e-08)

    column = lax.all_gather(normed, "z", axis=0, tiled=False)
    moments = jnp.stack([new_first, new_second]).reshape(2, 2, few, cols)
    mine, other = moments[:, 0], swap(moments[:, 1], "xh")
    moments = jnp.where(
        xh == 0, jnp.concatenate([mine, other], axis=1), jnp.concatenate([other, mine], axis=1)
    )

    back_part = rotate_back(me, column, basis, peers)
    back_part = exchange(back_part.reshape((-1,) + back_part.shape[2:]), ("xl", "core", "y"))
    back_part = back_part.reshape((4, peers) + back_part.shape[1:])
    back_copies = sum_and_copy(jnp.zeros_like(me), back_part, 2 * peers)
    got = exchange(back_copies, COL).reshape((2, peers) + back_copies.shape[1:])
    new_weight, direction = finish(got, left_basis, master_weight)
    return (new_weight, direction, moments[0], moments[1])


def solution(mesh):
    fine = Mesh(mesh.devices.reshape(12, 2, 2, 2, 8), ROW + COL)
    in_specs = (P(COL, ROW), P(COL, ROW), P(ROW, COL), P(ROW, COL), P(COL, None), P(ROW, COL))
    out_specs = (P(COL, ROW), P(COL, ROW), P(ROW, COL), P(ROW, COL))
    return jax.shard_map(shards, mesh=fine, in_specs=in_specs, out_specs=out_specs, check_vma=False)
```
